128 devices in a mesh: wide: 16 (over z_hi, x, core), narrow: 8 (over z_lo, y).
Axes of the slice: x: 4, y: 4, z: 4 (z_hi: 2, z_lo: 2; z = z_hi * 2 + z_lo), core: 2. Of those that a mesh axis runs over, the one named last changes fastest.
Arguments:
- tokens: bfloat16 [1536, 8192], P('wide', 'narrow'), may hold values from -6 to 6
- gate_up: bfloat16 [2, 28672, 8192], P(None, ('narrow', 'wide')), may hold values from -0.0625 to 0.0625
- down_weight: bfloat16 [28672, 8192], P(('narrow', 'wide')), may hold values from -0.125 to 0.125
Outputs:
- ffn_out: float32 [1536, 8192], P('wide', 'narrow')
The draws below stay inside these ranges and needn't reach their ends.
All inputs are finite; a program needn't handle non-finite values.
Results may differ from the reference program's by a relative error of at most 0.0029.
Values may be sent and summed in bfloat16 or wider, within the bound.
No kernel may reach another device: no remote copies, remote signals or barrier semaphores. Data moves between devices by JAX's collectives and lax.ppermute only.
A program may use at most 192 MiB of HBM per device.

```python
import jax
import jax.numpy as jnp

D = 8192
FF = 28672
TOKENS = 1536


def with_spikes(entries, key, source, target, shards_of, factor):
    owner, partner = [(jnp.arange(entries.shape[position]) // (entries.shape[position] // shards_of)).reshape([-1 if axis == position else 1 for axis in range(entries.ndim)]) for position in (source, target)]
    chosen = jax.random.permutation(key, shards_of)[partner]
    strong = (owner == chosen) | (owner == (partner + shards_of // 2) % shards_of)
    return jnp.where(strong, factor * entries, entries)


def block_scale(stream_key, extent, split, least, largest):
    level, own = 1.0, jax.random.fold_in(stream_key, 6)
    for position, blocks in split:
        steps = jnp.exp(jax.random.uniform(jax.random.fold_in(own, position), (blocks,), jnp.float32, least / len(split), largest / len(split)))
        level = level * jnp.repeat(steps, extent[position] // blocks).reshape([-1 if axis == position else 1 for axis in range(len(extent))])
    return level


def scatter_about(own_key, shape, width, bound, cuts=(), dtype=jnp.bfloat16):
    values = jax.random.normal(own_key, shape, jnp.float32) * width
    if len(cuts) > 0:
        values = block_scale(own_key, shape, cuts, -0.22, 0.18) * values
    return jnp.clip(values, min=-bound, max=bound).astype(dtype)


def noise_with(stream_key, shape, width, limit, pieces, heavy, dtype=jnp.bfloat16):
    entries = width * jax.random.normal(stream_key, shape, jnp.float32)
    if pieces:
        entries = entries * block_scale(stream_key, shape, pieces, -0.22, 0.18)
    return jnp.clip(with_spikes(entries, jax.random.fold_in(stream_key, 3), *heavy), -limit, limit).astype(dtype)


def setup_inputs(seed: int = 0) -> dict:
    arg_keys = jax.random.split(jax.random.key(seed), 4)
    tokens = scatter_about(arg_keys[0], (TOKENS, D), 1.0, 6.0, ((0, 16), (1, 8)))
    gate_up = scatter_about(arg_keys[1], (2, FF, D), D ** -0.5, 0.0625, ((1, 128),))
    down_weight = noise_with(arg_keys[2], (FF, D), FF ** -0.5, 0.125, ((0, 128),), (0, 1, 128, 5.5))
    return dict(tokens=tokens, gate_up=gate_up, down_weight=down_weight)


def reference(tokens, gate_up, down_weight):
    gate_sum = jnp.dot(tokens, gate_up[0].T, preferred_element_type=jnp.float32)
    up_sum = jnp.dot(tokens, gate_up[1].T, preferred_element_type=jnp.float32)
    hidden = (jax.nn.silu(gate_sum) * up_sum).astype(jnp.bfloat16)
    return jnp.dot(hidden, down_weight, preferred_element_type=jnp.float32)
```

```python
import jax
import jax.numpy as jnp
import numpy as np
from jax import lax
from jax.experimental import pallas as pl
from jax.experimental.pallas import tpu as pltpu
from jax.sharding import PartitionSpec as P

GRID = (2, 4, 2, 2, 4)
RINGS_A = (("z", "y"), ("y", "x"), ("x", "z"))
RINGS_B = (("x", "x"), ("z", "z"), ("y", "y"))
BOTH = ("wide", "narrow")


def partners(rings, flip):
    pairs = []
    for place in np.ndindex(*GRID):
        zh, x, core, zl, y = place
        ring = rings[core]
        if ring == "z":
            z = (2 * zh + zl) ^ flip
            zh, zl = z // 2, z % 2
        elif ring == "x":
            x ^= flip
        elif ring == "y":
            y ^= flip
        else:
            core ^= flip
        pairs.append(
            (
                int(np.ravel_multi_index(place, GRID)),
                int(np.ravel_multi_index((zh, x, core, zl, y), GRID)),
            )
        )
    return pairs


def swap(block, rings, flip):
    return lax.ppermute(block, BOTH, partners(rings, flip))


def gather_direct(block, rings):
    return jnp.stack([block] + [swap(block, rings, flip) for flip in (1, 2, 3)], axis=1)


def gather_relay(block, rings):
    one, three = swap(block, rings, 1), swap(block, rings, 3)
    return block, one, swap(one[0], rings, 3), swap(three[1], rings, 1), three


def column_block(place, step):
    return (place[1] ^ (step // 4)) * 4 + (place[2] ^ (step % 4))


def hidden_kernel(place, *refs):
    parts, (w_own, w_other), (h_own, h_other) = refs[:10], refs[10:12], refs[12:14]
    xa, xb, xk, acc, sems = refs[14:]
    step = pl.program_id(0)
    core = place[0]
    rows_a, rows_b = xa.shape[-2], xb.shape[-2]

    @pl.when(step == 0)
    def _():
        copies = []
        for stream, dest in enumerate((xa, xb)):
            own, one, two_a, two_b, three = parts[5 * stream : 5 * stream + 5]
            pairs = (
                (own, dest.at[0]),
                (one, dest.at[1]),
                (two_a, dest.at[2, 0]),
                (two_b, dest.at[2, 1]),
                (three, dest.at[3]),
            )
            for i, (src, dst) in enumerate(pairs):
                copies.append(pltpu.make_async_copy(src, dst, sems.at[5 * stream + i]))
        for copy in copies:
            copy.start()
        for copy in copies:
            copy.wait()
        acc[...] = jnp.zeros_like(acc)

    zl, y = step // 4, step % 4
    for zh in range(2):
        z = 2 * zh + zl
        for x in range(4):
            for half in range(2):
                row = (zh * 4 + x) * 2 + half
                b = jnp.where(core == 0, x, z)
                d2 = jnp.where(core == 0, y, x)
                d1 = jnp.where(core == 0, z, y)
                xk[pl.ds(row * rows_a, rows_a), :] = xa[b, half, d2 * 4 + d1]
                xk[pl.ds(16 * rows_a + row * rows_b, rows_b), :] = xb[y, half, z * 4 + x]

    total = xk.shape[0]
    chunk = total // 3

    def body(i, carry):
        rows = pl.ds(pl.multiple_of(i * chunk, chunk), chunk)
        lhs = xk[rows, :]
        for part, w in enumerate((w_own, w_other)):
            for which in range(2):
                acc[2 * part + which, rows, :] += lax.dot_general(
                    lhs, w[which], (((1,), (1,)), ((), ())), preferred_element_type=jnp.float32
                )
        return carry

    lax.fori_loop(0, 3, body, 0)

    @pl.when(step == 7)
    def _():
        for part, h in enumerate((h_own, h_other)):
            gate, up = acc[2 * part], acc[2 * part + 1]
            h[...] = (gate / (1 + jnp.exp(-gate)) * up).astype(jnp.bfloat16)


def hidden_call(place, parts, w_own, w_other):
    own_a, own_b = parts[0], parts[5]
    rows_a, rows_b, cols = own_a.shape[-2], own_b.shape[-2], own_a.shape[-1]
    total = 16 * (rows_a + rows_b)
    width = w_own.shape[1]
    w_spec = pl.BlockSpec((2, width, cols), lambda i, p: (0, 0, column_block(p, i)))
    h_spec = pl.BlockSpec((total, width), lambda i, p: (0, 0))
    return pl.pallas_call(
        hidden_kernel,
        out_shape=[jax.ShapeDtypeStruct((total, width), jnp.bfloat16)] * 2,
        grid_spec=pltpu.PrefetchScalarGridSpec(
            num_scalar_prefetch=1,
            grid=(8,),
            in_specs=[pl.BlockSpec(memory_space=pl.ANY)] * 10 + [w_spec, w_spec],
            out_specs=[h_spec, h_spec],
            scratch_shapes=[
                pltpu.VMEM((4, 2, 16, rows_a, cols), jnp.bfloat16),
                pltpu.VMEM((4, 2, 16, rows_b, cols), jnp.bfloat16),
                pltpu.VMEM((total, cols), jnp.bfloat16),
                pltpu.VMEM((4, total, width), jnp.float32),
                pltpu.SemaphoreType.DMA((10,)),
            ],
        ),
        compiler_params=pltpu.CompilerParams(
            dimension_semantics=("arbitrary",), vmem_limit_bytes=48 * 2**20
        ),
        cost_estimate=pl.CostEstimate(
            flops=2 * total * 8 * cols * 4 * width,
            bytes_accessed=2 * 8 * cols * (total + 4 * width),
            transcendentals=2 * total * width,
        ),
    )(place, *parts, w_own, w_other)


def output_kernel(place, h_own, h_other, d_own, d_other, *refs):
    outs, (narrow, wide, sems) = refs[:10], refs[10:]
    step = pl.program_id(0)
    core = place[0]
    slot = step % 2
    total, cols = wide.shape[1], wide.shape[2]
    rows_a, rows_b = outs[0].shape[-2], outs[5].shape[-2]

    def send(stream, b, half, index, row, sem, slot, act):
        rows = rows_b if stream else rows_a
        start = 16 * rows_a + row * rows if stream else row * rows
        own, e1, e3, f1, f3 = outs[5 * stream : 5 * stream + 5]
        src = narrow
        if b == 0:
            dst, src = own.at[half, index], wide
        elif b == 2:
            dst = (e1, e3)[half].at[0, index]
        elif b == 1:
            dst = f1.at[index] if half else e1.at[1, index]
        else:
            dst = e3.at[1, index] if half else f3.at[index]
        act(pltpu.make_async_copy(src.at[slot, pl.ds(start, rows)], dst, sems.at[slot, sem]))

    def move(step, slot, act):
        zl, y = step // 4, step % 4
        for zh in range(2):
            z = 2 * zh + zl
            for x in range(4):
                for half in range(2):
                    row = (zh * 4 + x) * 2 + half

                    @pl.when(core == 0)
                    def _():
                        send(0, x, half, y * 4 + z, row, row, slot, act)

                    for low in range(2):

                        @pl.when((core == 1) & (zl == low))
                        def _():
                            send(0, 2 * zh + low, half, x * 4 + y, row, row, slot, act)

                    for near in range(4):

                        @pl.when(y == near)
                        def _():
                            send(1, near, half, z * 4 + x, row, 16 + row, slot, act)

    @pl.when(step >= 2)
    def _():
        move(step - 2, slot, lambda copy: copy.wait())

    chunk = total // 3

    def body(i, carry):
        rows = pl.ds(pl.multiple_of(i * chunk, chunk), chunk)
        value = jnp.dot(h_own[rows, :], d_own[...], preferred_element_type=jnp.float32)
        value += jnp.dot(h_other[rows, :], d_other[...], preferred_element_type=jnp.float32)
        wide[slot, rows, :] = value
        narrow[slot, rows, :] = value.astype(jnp.bfloat16)
        return carry

    lax.fori_loop(0, 3, body, 0)
    move(step, slot, lambda copy: copy.start())

    @pl.when(step == 7)
    def _():
        move(step - 1, 1 - slot, lambda copy: copy.wait())
        move(step, slot, lambda copy: copy.wait())


def output_call(place, h_own, h_other, d_own, d_other, rows_a, rows_b):
    total, width = h_own.shape
    cols = d_own.shape[1] // 8
    h_spec = pl.BlockSpec((total, width), lambda i, p: (0, 0))
    d_spec = pl.BlockSpec((width, cols), lambda i, p: (0, column_block(p, i)))
    outs = []
    for rows in (rows_a, rows_b):
        outs += [
            jax.ShapeDtypeStruct((2, 16, rows, cols), jnp.float32),
            jax.ShapeDtypeStruct((2, 16, rows, cols), jnp.bfloat16),
            jax.ShapeDtypeStruct((2, 16, rows, cols), jnp.bfloat16),
            jax.ShapeDtypeStruct((16, rows, cols), jnp.bfloat16),
            jax.ShapeDtypeStruct((16, rows, cols), jnp.bfloat16),
        ]
    return pl.pallas_call(
        output_kernel,
        out_shape=outs,
        grid_spec=pltpu.PrefetchScalarGridSpec(
            num_scalar_prefetch=1,
            grid=(8,),
            in_specs=[h_spec, h_spec, d_spec, d_spec],
            out_specs=[pl.BlockSpec(memory_space=pl.ANY)] * 10,
            scratch_shapes=[
                pltpu.VMEM((2, total, cols), jnp.bfloat16),
                pltpu.VMEM((2, total, cols), jnp.float32),
                pltpu.SemaphoreType.DMA((2, 32)),
            ],
        ),
        compiler_params=pltpu.CompilerParams(
            dimension_semantics=("arbitrary",), vmem_limit_bytes=48 * 2**20
        ),
        cost_estimate=pl.CostEstimate(
            flops=2 * total * 8 * cols * 2 * width,
            bytes_accessed=2 * 8 * cols * (total + 2 * width),
            transcendentals=0,
        ),
    )(place, h_own, h_other, d_own, d_other)


def wider(block):
    return block.astype(jnp.float32)


def scatter_relay(blocks, rings):
    own, e1, e3, f1, f3 = blocks
    e1, e3 = swap(e1, rings, 1), swap(e3, rings, 3)
    f3 = swap((wider(f3) + wider(e1[0])).astype(jnp.bfloat16), rings, 3)
    f1 = swap((wider(f1) + wider(e3[0])).astype(jnp.bfloat16), rings, 1)
    return jnp.stack(
        [own[0] + wider(e1[1]) + wider(f3), own[1] + wider(f1) + wider(e3[1])]
    )


def scatter_direct(block, rings, dtype):
    total = block[:, 0]
    for flip in (1, 2, 3):
        total = total + wider(swap(block[:, flip].astype(dtype), rings, flip))
    return total


def shards(tokens, gate_up, down_weight):
    index = lax.axis_index("wide"), lax.axis_index("narrow")
    place = jnp.stack([index[0] % 2, index[1] // 4, index[1] % 4]).astype(jnp.int32)
    rows, cols = tokens.shape
    rows_a, rows_b = rows // 3, rows // 6
    streams = (
        (tokens[: 2 * rows_a].reshape(2, rows_a, cols), RINGS_A),
        (tokens[2 * rows_a :].reshape(2, rows_b, cols), RINGS_B),
    )
    w_other = swap(gate_up, ("core", "core"), 1)
    d_other = swap(down_weight, ("core", "core"), 1)
    firsts = [gather_direct(block, rings[0]) for block, rings in streams]
    seconds = [
        gather_direct(block, rings[1]).reshape(2, 16, block.shape[-2], cols)
        for block, (_, rings) in zip(firsts, streams)
    ]
    parts = [
        part
        for block, (_, rings) in zip(seconds, streams)
        for part in gather_relay(block, rings[2])
    ]
    h_own, h_other = hidden_call(place, parts, gate_up, w_other)
    outs = output_call(place, h_own, h_other, down_weight, d_other, rows_a, rows_b)
    sums = [
        scatter_relay(outs[5 * i : 5 * i + 5], rings[2]).reshape(2, 4, 4, -1, cols)
        for i, (_, rings) in enumerate(streams)
    ]
    sums = [
        scatter_direct(block, rings[1], jnp.bfloat16) for block, (_, rings) in zip(sums, streams)
    ]
    sums = [
        scatter_direct(block, rings[0], jnp.float32) for block, (_, rings) in zip(sums, streams)
    ]
    return jnp.concatenate([block.reshape(-1, cols) for block in sums])


def solution(mesh):
    return jax.shard_map(
        shards,
        mesh=mesh,
        in_specs=(
            P("wide", "narrow"),
            P(None, ("narrow", "wide"), None),
            P(("narrow", "wide"), None),
        ),
        out_specs=P("wide", "narrow"),
        check_vma=False,
    )
```

```python
import functools

import jax
import jax.numpy as jnp
import numpy as np
from jax import lax
from jax.experimental import pallas as pl
from jax.experimental.pallas import tpu as pltpu
from jax.sharding import PartitionSpec as P

GRID = (2, 4, 2, 2, 4)
RINGS_A = (("z", "y"), ("y", "x"), ("x", "z"))
RINGS_B = (("x", "x"), ("z", "z"), ("y", "y"))
BOTH = ("wide", "narrow")
UP, DOWN = (1, 1), (3, 3)
FIRST, SECOND = (1, 3), (3, 1)


def partners(rings, flips):
    pairs = []
    for place in np.ndindex(*GRID):
        zh, x, core, zl, y = place
        ring, flip = rings[core], flips[core]
        if ring == "z":
            z = (2 * zh + zl) ^ flip
            zh, zl = z // 2, z % 2
        elif ring == "x":
            x ^= flip
        elif ring == "y":
            y ^= flip
        else:
            core ^= flip
        pairs.append(
            (
                int(np.ravel_multi_index(place, GRID)),
                int(np.ravel_multi_index((zh, x, core, zl, y), GRID)),
            )
        )
    return pairs


def swap(block, rings, flips):
    return lax.ppermute(block, BOTH, partners(rings, flips))


def gather_direct(block, rings):
    return jnp.stack([block] + [swap(block, rings, (flip, flip)) for flip in (1, 2, 3)], axis=1)


def column_block(place, step):
    return (place[1] ^ (step // 4)) * 4 + (place[2] ^ (step % 4))


def resident(block):
    return pltpu.with_memory_space_constraint(block, pltpu.VMEM)


class Work:
    def __init__(self, places, hidden, output):
        self.places, self.hidden, self.output = places, hidden, output
        self.fresh = hidden and places == (0,)
        self.far = places == (2,)
        self.final = hidden and not self.fresh

    def __call__(self, place, tokens, gate_up, sums, hids, down):
        width, cols = (down or gate_up)[0].shape[-2], (down or gate_up)[0].shape[-1] // 8
        self.width, self.cols = width, cols
        self.size = size = self.rows
        total = 24 * size
        count = len(self.places)
        operands, out_shape, scratch = [place], [], []
        sum_shape = jax.ShapeDtypeStruct((4, total, width), jnp.float32)
        hid_shape = jax.ShapeDtypeStruct((total, width), jnp.bfloat16)
        vmem = pl.BlockSpec(memory_space=pltpu.VMEM)
        aliases = {}
        in_specs = [pl.BlockSpec(memory_space=pltpu.SMEM)]
        if self.hidden:
            operands += [*tokens[0], *tokens[1]]
            scratch += [
                pltpu.VMEM((count, 2, 16, size, cols), jnp.bfloat16),
                pltpu.VMEM((count, 1, 16, size, cols), jnp.bfloat16),
                pltpu.VMEM((2, total, cols), jnp.bfloat16),
                pltpu.SemaphoreType.DMA((4,)),
            ]
            out_shape.append(sum_shape)
            if self.final:
                out_shape += [hid_shape, hid_shape]
        in_specs += [pl.BlockSpec(memory_space=pl.ANY)] * (len(operands) - 1)
        if self.hidden:
            operands += gate_up
            in_specs += [vmem] * 2
            if not self.fresh:
                aliases[len(operands)] = 0
                operands.append(resident(sums))
                in_specs.append(vmem)
        if self.output:
            operands += [*down, *hids]
            in_specs += [vmem] * (2 + len(hids))
            half = jax.ShapeDtypeStruct((16, size, cols), jnp.bfloat16)
            whole = jax.ShapeDtypeStruct((2, 16, size, cols), jnp.bfloat16)
            out_shape += ([half] * 2 if self.far else [whole] * count) + [half] * count
        share = count / 4
        flops = 2 * total * 8 * cols * width * share * (4 * self.hidden + 2 * self.output)
        return pl.pallas_call(
            self.kernel,
            out_shape=out_shape,
            in_specs=in_specs,
            out_specs=[vmem] * len(out_shape),
            scratch_shapes=scratch,
            input_output_aliases=aliases,
            compiler_params=pltpu.CompilerParams(vmem_limit_bytes=28 * 2**20),
            cost_estimate=pl.CostEstimate(
                flops=int(1.5 * flops),
                bytes_accessed=2 * 8 * cols * width * (4 * self.hidden + 2 * self.output),
                transcendentals=0,
            ),
        )(*operands)

    def kernel(self, *refs):
        refs = list(refs)

        def take(count):
            taken = refs[:count]
            del refs[:count]
            return taken

        count = len(self.places)
        count_a = 2 if self.far else count
        (place,) = take(1)
        if self.hidden:
            tokens = take(count_a), take(count)
            gate_up = take(2)
            if not self.fresh:
                take(1)
        if self.output:
            down = take(2)
            hids = take(2) if self.hidden is False else None
            late = take(2) if self.hidden is False else None
        if self.hidden:
            (sums,) = take(1)
            if self.final:
                new = take(2)
        if self.output:
            outs = take(count_a), take(count)
        if self.hidden:
            xa, xb, rows_k, sem_x = take(4)
        if self.output and self.hidden:
            hids = late = new

        def where(step):
            return pl.ds(pl.multiple_of(column_block(place, step) * self.cols, self.cols), self.cols)

        def start(copies):
            for copy in copies:
                copy.start()

        def wait(copies):
            for copy in copies:
                copy.wait()

        if self.hidden:
            copies_x = []
            for stream, dest in enumerate((xa, xb)):
                for i, part in enumerate(tokens[stream]):
                    dst = dest.at[0, i] if self.far and stream == 0 else dest.at[i]
                    dst = dst.at[0] if stream else dst
                    copies_x.append(pltpu.make_async_copy(part, dst, sem_x.at[2 * stream + i]))
            start(copies_x)
            if self.fresh:
                sums[...] = jnp.zeros_like(sums)

        def run(core):
            steps = self.steps(core)
            if self.hidden:
                wait(copies_x)
                for step in steps:
                    self.hidden_step(core, step, xa, xb, gate_up, where(step), rows_k, sums)
            if self.final:
                for first, size in self.finished(core):
                    rows = pl.ds(first * self.size, size * self.size)
                    for part, h in enumerate(new):
                        gate, up = sums[2 * part, rows, :], sums[2 * part + 1, rows, :]
                        h[rows, :] = (gate / (1 + jnp.exp(-gate)) * up).astype(jnp.bfloat16)
            if self.output:
                for step in steps:
                    self.output_step(core, step, hids, late, down, where(step), outs)

        for core in range(2):
            pl.when(place[0] == core)(functools.partial(run, core))

    def steps(self, core):
        used = lambda zl, y: core == 0 or zl == self.places[0] % 2 or y in self.places
        return [4 * zl + y for zl in range(2) for y in range(4) if used(zl, y)]

    def finished(self, core):
        if self.far:
            return [(8, 4), (16, 8)] if core == 0 else [(8, 16)]
        return [(0, 8), (12, 4)] if core == 0 else [(0, 8)]

    def spans(self, core, step):
        zl, y = step // 4, step % 4
        found = []
        for i, near in enumerate(self.places):
            if core == 0:
                blocks = [(h, y * 4 + 2 * zh + zl) for zh in range(2) for h in range(2)]
                found.append((0, i, 4 * near, blocks))
            elif near % 2 == zl:
                blocks = [(h, x * 4 + y) for x in range(4) for h in range(2)]
                found.append((0, i, 8 * (near // 2), blocks))
        for i, near in enumerate(self.places if core == 0 else self.places[::-1]):
            if near == y:
                blocks = [(0, (2 * zh + zl) * 4 + x) for zh in range(2) for x in range(4)]
                found.append((1, i, 16, blocks))
        return found

    def hidden_step(self, core, step, xa, xb, gate_up, cols, rows_k, sums):
        slot, row, size, runs = step % 2, 0, self.size, []
        for stream, i, first, blocks in self.spans(core, step):
            source = (xa, xb)[stream]
            runs.append((row, first * size, size * len(blocks)))
            for half, index in blocks:
                rows_k[slot, pl.ds(row, size), :] = source[i, half, index]
                row += size
        lhs = rows_k[slot, pl.ds(0, row), :]
        for part in range(2):
            for which in range(2):
                value = lax.dot_general(
                    lhs,
                    gate_up[part][which, :, cols],
                    (((1,), (1,)), ((), ())),
                    preferred_element_type=jnp.float32,
                )
                for start, first, count in runs:
                    sums[2 * part + which, pl.ds(first, count), :] += value[start : start + count]

    def output_step(self, core, step, hids, late, down, cols, outs):
        size = self.size
        for stream, i, first, blocks in self.spans(core, step):
            rows = pl.ds(first * size, size * len(blocks))
            is_late = any(begin <= first < begin + count for begin, count in FAR.finished(core))
            own, other = late if is_late else hids
            value = jnp.dot(own[rows, :], down[0][:, cols], preferred_element_type=jnp.float32)
            value += jnp.dot(other[rows, :], down[1][:, cols], preferred_element_type=jnp.float32)
            for n, (half, index) in enumerate(blocks):
                piece = value[n * size : (n + 1) * size].astype(jnp.bfloat16)
                if stream:
                    outs[1][i][index] = piece
                elif self.far:
                    outs[0][half][index] = piece
                else:
                    outs[0][i][half, index] = piece


FAR = Work((2,), True, True)


def add_kernel(*refs):
    for target, other, out in zip(refs[0:6:2], refs[1:6:2], refs[6:]):
        total = target[...].astype(jnp.float32) + other[...].astype(jnp.float32)
        out[...] = total.astype(jnp.bfloat16)


def add_arrived(one, three, last, arrived):
    _, count, rows, cols = one.shape
    some = count // 4
    specs = [
        pl.BlockSpec((None, some, rows, cols), lambda n: (1, n, 0, 0)),
        pl.BlockSpec((None, some, rows, cols), lambda n: (0, n, 0, 0)),
        pl.BlockSpec((some, rows, cols), lambda n: (n, 0, 0)),
    ]
    blocks = (one, three, last)
    return pl.pallas_call(
        add_kernel,
        out_shape=[jax.ShapeDtypeStruct(block.shape, block.dtype) for block in blocks],
        grid=(4,),
        in_specs=[spec for own in specs for spec in (own, specs[2])],
        out_specs=specs,
        input_output_aliases={0: 0, 2: 1, 4: 2},
        compiler_params=pltpu.CompilerParams(vmem_limit_bytes=32 * 2**20),
    )(one, arrived[0], three, arrived[1], last, arrived[2])


def wider(block):
    return block.astype(jnp.float32)


def scatter_direct(block, rings, dtype):
    total = block[:, 0]
    for flip in (1, 2, 3):
        total = total + wider(swap(block[:, flip].astype(dtype), rings, (flip, flip)))
    return total


def shards(tokens, gate_up, down_weight):
    index = lax.axis_index("wide"), lax.axis_index("narrow")
    place = jnp.stack([index[0] % 2, index[1] // 4, index[1] % 4]).astype(jnp.int32)
    rows, cols = tokens.shape
    size = rows // 3
    Work.rows = size
    blocks = tokens[: 2 * size].reshape(2, size, cols), tokens[2 * size :].reshape(1, size, cols)
    rings = RINGS_A, RINGS_B
    cores = ("core", "core")

    blocks = [gather_direct(block, ring[0]) for block, ring in zip(blocks, rings)]
    blocks = lax.optimization_barrier(blocks)
    blocks = [gather_direct(block, ring[1]) for block, ring in zip(blocks, rings)]
    *blocks, gate_up, down_weight = lax.optimization_barrier((*blocks, gate_up, down_weight))
    own_a, own_b = blocks[0].reshape(2, 16, size, cols), blocks[1].reshape(16, size, cols)

    ring_a, ring_b = RINGS_A[2], RINGS_B[2]
    one_a, three_a = swap(own_a, ring_a, UP), swap(own_a, ring_a, DOWN)
    one_b, three_b = swap(own_b, ring_b, FIRST), swap(own_b, ring_b, SECOND)
    w = resident(gate_up), resident(swap(gate_up, cores, UP))
    (sums,) = Work((0,), True, False)(place, ([own_a], [own_b]), w, None, None, None)
    one_a, three_a, one_b, three_b, sums, down_weight = lax.optimization_barrier(
        (one_a, three_a, one_b, three_b, sums, down_weight)
    )
    two_b = swap(one_b, ring_b, SECOND)
    two_a = [swap(one_a[0], ring_a, DOWN), swap(three_a[1], ring_a, UP)]
    d = resident(down_weight), resident(swap(down_weight, cores, UP))
    sums, *hids = Work((1, 3), True, False)(
        place, ([one_a, three_a], [one_b, three_b]), w, sums, None, None
    )
    two_a, two_b, sums = lax.optimization_barrier((two_a, two_b, sums))
    _, *late, far_a0, far_a1, far_b = FAR(place, (two_a, [two_b]), w, sums, [], d)

    arrived = [
        swap(far_a1, ring_a, DOWN),
        swap(far_a0, ring_a, UP),
        swap(far_b, ring_b, FIRST),
    ]
    one_a, three_a, one_b, three_b = Work((1, 3), False, True)(
        place, None, None, None, [*hids, *late], d
    )
    one_b = swap(one_b, ring_b, FIRST)
    one_a, three_a, three_b = add_arrived(one_a, three_a, three_b, arrived)
    one_a, three_a = swap(one_a, ring_a, UP), swap(three_a, ring_a, DOWN)
    three_b = swap(three_b, ring_b, SECOND)
    own_a, own_b = Work((0,), False, True)(place, None, None, None, [*hids, *late], d)
    near = lax.optimization_barrier((own_a, one_a, three_a, own_b, one_b, three_b))
    blocks = [sum(wider(block) for block in near[3 * i : 3 * i + 3]) for i in range(2)]
    blocks = [block.reshape(-1, 4, 4, size, cols) for block in blocks]
    blocks = [scatter_direct(block, ring[1], jnp.bfloat16) for block, ring in zip(blocks, rings)]
    blocks = [scatter_direct(block, ring[0], jnp.float32) for block, ring in zip(blocks, rings)]
    return jnp.concatenate([block.reshape(-1, cols) for block in blocks])


def solution(mesh):
    return jax.shard_map(
        shards,
        mesh=mesh,
        in_specs=(
            P("wide", "narrow"),
            P(None, ("narrow", "wide"), None),
            P(("narrow", "wide"), None),
        ),
        out_specs=P("wide", "narrow"),
        check_vma=False,
    )
```

```python
import functools

import jax
import jax.numpy as jnp
import numpy as np
from jax import lax
from jax.experimental import pallas as pl
from jax.experimental.pallas import tpu as pltpu
from jax.sharding import PartitionSpec as P

GRID = (2, 4, 2, 2, 4)
RINGS_A = (("z", "y"), ("y", "x"), ("x", "z"))
RINGS_B = (("x", "x"), ("z", "z"), ("y", "y"))
RING = (RINGS_A[2], RINGS_A[2], RINGS_B[2])
FIRST = ((1, 1), (3, 3), (1, 3))
SECOND = ((3, 3), (1, 1), (3, 1))
BOTH = ("wide", "narrow")


def partners(rings, flips):
    pairs = []
    for place in np.ndindex(*GRID):
        zh, x, core, zl, y = place
        ring, flip = rings[core], flips[core]
        if ring == "z":
            z = (2 * zh + zl) ^ flip
            zh, zl = z // 2, z % 2
        elif ring == "x":
            x ^= flip
        elif ring == "y":
            y ^= flip
        else:
            core ^= flip
        pairs.append(
            (
                int(np.ravel_multi_index(place, GRID)),
                int(np.ravel_multi_index((zh, x, core, zl, y), GRID)),
            )
        )
    return pairs


def swap(block, rings, flips):
    return lax.ppermute(block, BOTH, partners(rings, flips))


def tie(*blocks):
    return lax.optimization_barrier(blocks)


def direct(pair, single, phase):
    pairs, singles = {}, {}
    for flip in (2, 1, 3):
        pairs[flip] = swap(pair[flip], RINGS_A[phase], (flip, flip))
    for flip in (2, 3):
        singles[flip] = swap(single[flip], RINGS_B[phase], (flip, flip))
    last, pairs[1] = tie(single[1], pairs[1])
    singles[1] = swap(last, RINGS_B[phase], (1, 1))
    return pairs, singles


VMEM_LIMIT = 14 * 2**20


def column_block(place, step):
    return (place[1] ^ (step // 4)) * 4 + (place[2] ^ (step % 4))


def resident(block):
    return pltpu.with_memory_space_constraint(block, pltpu.VMEM)


class Work:
    def __init__(self, places, hidden, output):
        self.places, self.hidden, self.output = places, hidden, output
        self.fresh = hidden and places == (0,)
        self.far = places == (2,)
        self.final = hidden and not self.fresh

    def __call__(self, place, tokens, gate_up, sums, hids, down):
        width, cols = (down or gate_up)[0].shape[-2], (down or gate_up)[0].shape[-1] // 8
        self.width, self.cols = width, cols
        size = self.size
        total = 24 * size
        count = 3 * len(self.places)
        aliases = {}
        operands, out_shape, scratch = [place], [], []
        sum_shape = jax.ShapeDtypeStruct((4, total, width), jnp.float32)
        hid_shape = jax.ShapeDtypeStruct((total, width), jnp.bfloat16)
        if self.hidden:
            operands += [resident(block) for block in tokens]
            operands += [resident(block) for block in gate_up]
            if not self.fresh:
                aliases[len(operands)] = 0
                operands.append(resident(sums))
            scratch.append(pltpu.VMEM((2, total, cols), jnp.bfloat16))
            out_shape.append(sum_shape)
            if self.final:
                out_shape += [hid_shape, hid_shape]
        if self.output:
            operands += [resident(block) for block in (*down, *hids)]
            out_shape += [jax.ShapeDtypeStruct((16, size, cols), jnp.bfloat16)] * count
        vmem = pl.BlockSpec(memory_space=pltpu.VMEM)
        return pl.pallas_call(
            self.kernel,
            out_shape=out_shape,
            in_specs=[pl.BlockSpec(memory_space=pltpu.SMEM)] + [vmem] * (len(operands) - 1),
            out_specs=[vmem] * len(out_shape),
            scratch_shapes=scratch,
            input_output_aliases=aliases,
            compiler_params=pltpu.CompilerParams(vmem_limit_bytes=VMEM_LIMIT),
            cost_estimate=pl.CostEstimate(flops=0, bytes_accessed=2**20, transcendentals=0),
        )(*operands)

    def kernel(self, *refs):
        refs = list(refs)

        def take(count):
            taken = refs[:count]
            del refs[:count]
            return taken

        count = 3 * len(self.places)
        (place,) = take(1)
        if self.hidden:
            tokens, gate_up = take(count), take(2)
            if not self.fresh:
                take(1)
        if self.output:
            down = take(2)
            if not self.hidden:
                hids, late = take(2), take(2)
        if self.hidden:
            (sums,) = take(1)
            if self.final:
                new = take(2)
        if self.output:
            outs = take(count)
            if self.hidden:
                hids = late = new
        if self.hidden:
            (rows_k,) = take(1)

        def where(step):
            return pl.ds(pl.multiple_of(column_block(place, step) * self.cols, self.cols), self.cols)

        if self.fresh:
            sums[...] = jnp.zeros_like(sums)

        def run(core):
            steps = self.steps(core)
            if self.hidden:
                for step in steps:
                    self.hidden_step(core, step, tokens, gate_up, where(step), rows_k, sums)
            if self.final:
                for first, count in self.finished(core):
                    rows = pl.ds(first * self.size, count * self.size)
                    for part, h in enumerate(new):
                        gate, up = sums[2 * part, rows, :], sums[2 * part + 1, rows, :]
                        h[rows, :] = (gate / (1 + jnp.exp(-gate)) * up).astype(jnp.bfloat16)
            if self.output:
                for step in steps:
                    self.output_step(core, step, hids, late, down, where(step), outs)

        for core in range(2):
            pl.when(place[0] == core)(functools.partial(run, core))

    def steps(self, core):
        used = lambda zl, y: core == 0 or zl == self.places[0] % 2 or y in self.places
        return [4 * zl + y for zl in range(2) for y in range(4) if used(zl, y)]

    def finished(self, core):
        if self.far:
            return [(4, 2), (12, 2), (16, 8)] if core == 0 else [(4, 4), (12, 12)]
        return [(0, 4), (6, 6), (14, 2)] if core == 0 else [(0, 4), (8, 4)]

    def spans(self, core, step):
        zl, y = step // 4, step % 4
        found = []
        for stream in range(3):
            places = self.places
            if len(places) == 2:
                places = FIRST[stream][core], SECOND[stream][core]
            for i, near in enumerate(places):
                which = stream * len(places) + i
                if stream == 2:
                    if near == y:
                        blocks = [(2 * zh + zl) * 4 + x for zh in range(2) for x in range(4)]
                        found.append((which, 16, blocks))
                elif core == 0:
                    blocks = [y * 4 + 2 * zh + zl for zh in range(2)]
                    found.append((which, 8 * stream + 2 * near, blocks))
                elif near % 2 == zl:
                    blocks = [x * 4 + y for x in range(4)]
                    found.append((which, 8 * stream + 4 * (near // 2), blocks))
        return found

    def hidden_step(self, core, step, tokens, gate_up, cols, rows_k, sums):
        slot, row, size, runs = step % 2, 0, self.size, []
        for which, first, blocks in self.spans(core, step):
            runs.append((row, first * size, size * len(blocks)))
            for index in blocks:
                rows_k[slot, pl.ds(row, size), :] = tokens[which][index]
                row += size
        lhs = rows_k[slot, pl.ds(0, row), :]
        for part in range(2):
            for which in range(2):
                value = lax.dot_general(
                    lhs,
                    gate_up[part][which, :, cols],
                    (((1,), (1,)), ((), ())),
                    preferred_element_type=jnp.float32,
                )
                for start, first, count in runs:
                    sums[2 * part + which, pl.ds(first, count), :] += value[start : start + count]

    def output_step(self, core, step, hids, late, down, cols, outs):
        size = self.size
        spans, lhs = self.spans(core, step), ([], [])
        for _, first, blocks in spans:
            rows = pl.ds(first * size, size * len(blocks))
            is_late = any(begin <= first < begin + count for begin, count in FAR.finished(core))
            for part, hid in enumerate(late if is_late else hids):
                lhs[part].append(hid[rows, :])
        value = sum(
            jnp.dot(jnp.concatenate(rows), down[part][:, cols], preferred_element_type=jnp.float32)
            for part, rows in enumerate(lhs)
        )
        row = 0
        for which, _, blocks in spans:
            for index in blocks:
                outs[which][index] = value[row : row + size].astype(jnp.bfloat16)
                row += size


FAR = Work((2,), True, True)


def add_kernel(*refs):
    count = len(refs) // 3
    for block, other, out in zip(refs[:count], refs[count:], refs[2 * count :]):
        total = block[...].astype(jnp.float32) + other[...].astype(jnp.float32)
        out[...] = total.astype(jnp.bfloat16)


def add(blocks, others):
    count, rows, cols = blocks[0].shape
    spec = pl.BlockSpec((count // 4, rows, cols), lambda n: (n, 0, 0))
    return pl.pallas_call(
        add_kernel,
        out_shape=[jax.ShapeDtypeStruct(block.shape, block.dtype) for block in blocks],
        grid=(4,),
        in_specs=[spec] * (2 * len(blocks)),
        out_specs=[spec] * len(blocks),
        input_output_aliases={i: i for i in range(len(blocks))},
        compiler_params=pltpu.CompilerParams(vmem_limit_bytes=VMEM_LIMIT),
    )(*blocks, *others)


def wider(block):
    return block.astype(jnp.float32)


def each(blocks, flips):
    return [swap(block, ring, flip) for block, ring, flip in zip(blocks, RING, flips)]


def shards(tokens, gate_up, down_weight):
    index = lax.axis_index("wide"), lax.axis_index("narrow")
    place = jnp.stack([index[0] % 2, index[1] // 4, index[1] % 4]).astype(jnp.int32)
    rows, cols = tokens.shape
    Work.size = size = rows // 3
    cores = ("core", "core")
    w_other = swap(gate_up, cores, (1, 1))
    pair, single = tokens[: 2 * size].reshape(2, size, cols), tokens[2 * size :].reshape(1, size, cols)
    pairs, singles = direct([pair] * 4, [single] * 4, 0)
    pair = jnp.stack([pair] + [pairs[flip] for flip in (1, 2, 3)], axis=1)
    single = jnp.stack([single] + [singles[flip] for flip in (1, 2, 3)], axis=1)
    pair, single, w_other = tie(pair, single, w_other)
    w = gate_up, w_other
    pairs, singles = direct([pair] * 4, [single] * 4, 1)
    pairs, singles = [[own] + [got[flip] for flip in (1, 2, 3)] for own, got in ((pair, pairs), (single, singles))]
    own = [jnp.concatenate([block[i] for block in pairs]) for i in range(2)]
    own.append(jnp.concatenate([block[0] for block in singles]))
    own = list(tie(*own))

    first = each(own, FIRST)
    own_2, first[2] = tie(own[2], first[2])
    second = each([*own[:2], own_2], SECOND)
    (sums,) = Work((0,), True, False)(place, own, w, None, None, None)
    first[0], first[1], first[2], second[0], second[1], second[2], sums, down_weight = tie(
        *first, *second, sums, down_weight
    )
    relay = each(first, SECOND)
    d = down_weight, swap(down_weight, cores, (1, 1))
    near = [block for both in zip(first, second) for block in both]
    sums, *hids = Work((1, 3), True, False)(place, near, w, sums, None, None)
    *relay, sums = tie(*relay, sums)
    _, own_hid, other_hid, *far = FAR(place, relay, w, sums, [], d)
    hids += [own_hid, other_hid]

    arrived = each(far, FIRST)
    near = Work((1, 3), False, True)(place, None, None, None, hids, d)
    first, second = near[0::2], near[1::2]
    first = each(first, FIRST)
    second = each(add(second, arrived), SECOND)
    own = Work((0,), False, True)(place, None, None, None, hids, d)
    own, first, second = tie(own, first, second)
    parts = [
        sum(wider(block) for block in blocks).reshape(4, 4, size, cols)
        for blocks in zip(own, first, second)
    ]
    pair, single = jnp.stack(parts[:2]), parts[2][None]
    for phase, dtype in ((1, jnp.bfloat16), (0, jnp.float32)):
        out = [
            [block[:, 0]] + [block[:, flip].astype(dtype) for flip in (1, 2, 3)]
            for block in (pair, single)
        ]
        out = tie(*out)
        pairs, singles = direct(*out, phase)
        pair = out[0][0] + wider(pairs[1]) + wider(pairs[2]) + wider(pairs[3])
        single = out[1][0] + wider(singles[1]) + wider(singles[2]) + wider(singles[3])
    return jnp.concatenate([pair.reshape(-1, cols), single.reshape(-1, cols)])


def solution(mesh):
    return jax.shard_map(
        shards,
        mesh=mesh,
        in_specs=(
            P("wide", "narrow"),
            P(None, ("narrow", "wide"), None),
            P(("narrow", "wide"), None),
        ),
        out_specs=P("wide", "narrow"),
        check_vma=False,
    )
```

```python
import functools

import jax
import jax.numpy as jnp
import numpy as np
from jax import lax
from jax.experimental import pallas as pl
from jax.experimental.pallas import tpu as pltpu
from jax.sharding import PartitionSpec as P

GRID = (2, 4, 2, 2, 4)
RINGS_A = (("z", "y"), ("y", "x"), ("x", "z"))
RINGS_B = (("x", "x"), ("z", "z"), ("y", "y"))
RING = (RINGS_A[2], RINGS_A[2], RINGS_B[2])
FIRST = ((1, 1), (3, 3), (1, 3))
SECOND = ((3, 3), (1, 1), (3, 1))
BOTH = ("wide", "narrow")


def partners(rings, flips):
    pairs = []
    for place in np.ndindex(*GRID):
        zh, x, core, zl, y = place
        ring, flip = rings[core], flips[core]
        if ring == "z":
            z = (2 * zh + zl) ^ flip
            zh, zl = z // 2, z % 2
        elif ring == "x":
            x ^= flip
        elif ring == "y":
            y ^= flip
        else:
            core ^= flip
        pairs.append(
            (
                int(np.ravel_multi_index(place, GRID)),
                int(np.ravel_multi_index((zh, x, core, zl, y), GRID)),
            )
        )
    return pairs


def swap(block, rings, flips):
    return lax.ppermute(block, BOTH, partners(rings, flips))


def tie(*blocks):
    return lax.optimization_barrier(blocks)


def direct(pair, single, phase):
    pairs, singles = {}, {}
    for flip in (2, 1, 3):
        pairs[flip] = swap(pair[flip], RINGS_A[phase], (flip, flip))
    for flip in (2, 3):
        singles[flip] = swap(single[flip], RINGS_B[phase], (flip, flip))
    last, pairs[1] = tie(single[1], pairs[1])
    singles[1] = swap(last, RINGS_B[phase], (1, 1))
    return pairs, singles


VMEM_LIMIT = 10 * 2**20


def column_block(place, step):
    return (place[1] ^ (step // 4)) * 4 + (place[2] ^ (step % 4))


def resident(block):
    return pltpu.with_memory_space_constraint(block, pltpu.VMEM)


class Work:
    def __init__(self, places, hidden, output):
        self.places, self.hidden, self.output = places, hidden, output
        self.fresh = hidden and places == (0,)
        self.far = places == (2,)
        self.final = hidden and not self.fresh

    def __call__(self, place, tokens, gate_up, sums, hids, down, *after):
        width, cols = (down or gate_up)[0].shape[-2], (down or gate_up)[0].shape[-1] // 8
        self.width, self.cols = width, cols
        size = self.size
        total = 24 * size
        count = 3 * len(self.places)
        aliases = {}
        operands, out_shape, scratch = [place], [], []
        sum_shape = jax.ShapeDtypeStruct((4, total, width), jnp.float32)
        hid_shape = jax.ShapeDtypeStruct((total, width), jnp.bfloat16)
        if self.hidden:
            operands += [resident(block) for block in tokens]
            operands += [resident(block) for block in gate_up]
            if not self.fresh:
                aliases[len(operands)] = 0
                operands.append(resident(sums))
            scratch.append(pltpu.VMEM((1, total, cols), jnp.bfloat16))
            out_shape.append(sum_shape)
            if self.final:
                out_shape += [hid_shape, hid_shape]
        if self.output:
            operands += [resident(block) for block in (*down, *hids)]
            out_shape += [jax.ShapeDtypeStruct((16, size, cols), jnp.bfloat16)] * count
        operands += after
        self.after = len(after)
        vmem = pl.BlockSpec(memory_space=pltpu.VMEM)
        return pl.pallas_call(
            self.kernel,
            out_shape=out_shape,
            in_specs=[pl.BlockSpec(memory_space=pltpu.SMEM)] + [vmem] * (len(operands) - 1),
            out_specs=[vmem] * len(out_shape),
            scratch_shapes=scratch,
            input_output_aliases=aliases,
            compiler_params=pltpu.CompilerParams(vmem_limit_bytes=VMEM_LIMIT),
            cost_estimate=pl.CostEstimate(flops=2**36, bytes_accessed=2**27, transcendentals=0),
        )(*operands)

    def kernel(self, *refs):
        refs = list(refs)

        def take(count):
            taken = refs[:count]
            del refs[:count]
            return taken

        count = 3 * len(self.places)
        (place,) = take(1)
        if self.hidden:
            tokens, gate_up = take(count), take(2)
            if not self.fresh:
                take(1)
        if self.output:
            down = take(2)
            if not self.hidden:
                hids, late = take(2), take(2)
        take(self.after)
        if self.hidden:
            (sums,) = take(1)
            if self.final:
                new = take(2)
        if self.output:
            outs = take(count)
            if self.hidden:
                hids = late = new
        if self.hidden:
            (rows_k,) = take(1)

        def where(step):
            return pl.ds(pl.multiple_of(column_block(place, step) * self.cols, self.cols), self.cols)

        if self.fresh:
            sums[...] = jnp.zeros_like(sums)

        def run(core):
            steps = self.steps(core)
            if self.hidden:
                for step in steps:
                    self.hidden_step(core, step, tokens, gate_up, where(step), rows_k, sums)
            if self.final:
                for first, count in self.finished(core):
                    rows = pl.ds(first * self.size, count * self.size)
                    for part, h in enumerate(new):
                        gate, up = sums[2 * part, rows, :], sums[2 * part + 1, rows, :]
                        h[rows, :] = (gate / (1 + jnp.exp(-gate)) * up).astype(jnp.bfloat16)
            if self.output:
                for step in steps:
                    self.output_step(core, step, hids, late, down, where(step), outs)

        for core in range(2):
            pl.when(place[0] == core)(functools.partial(run, core))

    def steps(self, core):
        used = lambda zl, y: core == 0 or zl == self.places[0] % 2 or y in self.places
        return [4 * zl + y for zl in range(2) for y in range(4) if used(zl, y)]

    def finished(self, core):
        if self.far:
            return [(4, 2), (12, 2), (16, 8)] if core == 0 else [(4, 4), (12, 12)]
        return [(0, 4), (6, 6), (14, 2)] if core == 0 else [(0, 4), (8, 4)]

    def spans(self, core, step):
        zl, y = step // 4, step % 4
        found = []
        for stream in range(3):
            places = self.places
            if len(places) == 2:
                places = FIRST[stream][core], SECOND[stream][core]
            for i, near in enumerate(places):
                which = stream * len(places) + i
                if stream == 2:
                    if near == y:
                        blocks = [(2 * zh + zl) * 4 + x for zh in range(2) for x in range(4)]
                        found.append((which, 16, blocks))
                elif core == 0:
                    blocks = [y * 4 + 2 * zh + zl for zh in range(2)]
                    found.append((which, 8 * stream + 2 * near, blocks))
                elif near % 2 == zl:
                    blocks = [x * 4 + y for x in range(4)]
                    found.append((which, 8 * stream + 4 * (near // 2), blocks))
        return found

    def hidden_step(self, core, step, tokens, gate_up, cols, rows_k, sums):
        slot, row, size, runs = 0, 0, self.size, []
        for which, first, blocks in self.spans(core, step):
            runs.append((row, first * size, size * len(blocks)))
            for index in blocks:
                rows_k[slot, pl.ds(row, size), :] = tokens[which][index]
                row += size
        lhs = rows_k[slot, pl.ds(0, row), :]
        for part in range(2):
            for which in range(2):
                value = lax.dot_general(
                    lhs,
                    gate_up[part][which, :, cols],
                    (((1,), (1,)), ((), ())),
                    preferred_element_type=jnp.float32,
                )
                for start, first, count in runs:
                    sums[2 * part + which, pl.ds(first, count), :] += value[start : start + count]

    def output_step(self, core, step, hids, late, down, cols, outs):
        size = self.size
        spans, lhs = self.spans(core, step), ([], [])
        for _, first, blocks in spans:
            rows = pl.ds(first * size, size * len(blocks))
            is_late = any(begin <= first < begin + count for begin, count in FAR.finished(core))
            for part, hid in enumerate(late if is_late else hids):
                lhs[part].append(hid[rows, :])
        value = sum(
            jnp.dot(jnp.concatenate(rows), down[part][:, cols], preferred_element_type=jnp.float32)
            for part, rows in enumerate(lhs)
        )
        row = 0
        for which, _, blocks in spans:
            for index in blocks:
                outs[which][index] = value[row : row + size].astype(jnp.bfloat16)
                row += size


FAR = Work((2,), True, True)


def add_kernel(*refs):
    count = len(refs) // 3
    for block, other, out in zip(refs[:count], refs[count:], refs[2 * count :]):
        total = block[...].astype(jnp.float32) + other[...].astype(jnp.float32)
        out[...] = total.astype(jnp.bfloat16)


def add(blocks, others):
    count, rows, cols = blocks[0].shape
    spec = pl.BlockSpec((count // 4, rows, cols), lambda n: (n, 0, 0))
    return pl.pallas_call(
        add_kernel,
        out_shape=[jax.ShapeDtypeStruct(block.shape, block.dtype) for block in blocks],
        grid=(4,),
        in_specs=[spec] * (2 * len(blocks)),
        out_specs=[spec] * len(blocks),
        input_output_aliases={i: i for i in range(len(blocks))},
        compiler_params=pltpu.CompilerParams(vmem_limit_bytes=VMEM_LIMIT),
    )(*blocks, *others)


def wider(block):
    return block.astype(jnp.float32)


def each(blocks, flips):
    return [swap(block, ring, flip) for block, ring, flip in zip(blocks, RING, flips)]


def shards(tokens, gate_up, down_weight):
    index = lax.axis_index("wide"), lax.axis_index("narrow")
    place = jnp.stack([index[0] % 2, index[1] // 4, index[1] % 4]).astype(jnp.int32)
    rows, cols = tokens.shape
    Work.size = size = rows // 3
    cores = ("core", "core")
    w_other = swap(gate_up, cores, (1, 1))
    pair, single = tokens[: 2 * size].reshape(2, size, cols), tokens[2 * size :].reshape(1, size, cols)
    pairs, singles = direct([pair] * 4, [single] * 4, 0)
    pair = jnp.stack([pair] + [pairs[flip] for flip in (1, 2, 3)], axis=1)
    single = jnp.stack([single] + [singles[flip] for flip in (1, 2, 3)], axis=1)
    pair, single, arrived = tie(pair, single, w_other[0, :16, :128])
    w = gate_up, w_other
    pairs, singles = direct([pair] * 4, [single] * 4, 1)
    pairs, singles = [[own] + [got[flip] for flip in (1, 2, 3)] for own, got in ((pair, pairs), (single, singles))]
    own = [jnp.concatenate([block[i] for block in pairs]) for i in range(2)]
    own.append(jnp.concatenate([block[0] for block in singles]))
    own = list(tie(*own))

    first = each(own, FIRST)
    own_2, first[2] = tie(own[2], first[2])
    second = each([*own[:2], own_2], SECOND)
    (sums,) = Work((0,), True, False)(place, own, w, None, None, None, arrived)
    first[0], first[1], first[2], second[0], second[1], second[2], sums, down_weight = tie(
        *first, *second, sums, down_weight
    )
    relay = each(first, SECOND)
    d = down_weight, swap(down_weight, cores, (1, 1))
    near = [block for both in zip(first, second) for block in both]
    sums, *hids = Work((1, 3), True, False)(place, near, w, sums, None, None)
    *relay, sums = tie(*relay, sums)
    _, own_hid, other_hid, *far = FAR(place, relay, w, sums, [], d)
    hids += [own_hid, other_hid]

    arrived = each(far, FIRST)
    near = Work((1, 3), False, True)(place, None, None, None, hids, d)
    first, second = near[0::2], near[1::2]
    first = each(first, FIRST)
    second = each(add(second, arrived), SECOND)
    own = Work((0,), False, True)(place, None, None, None, hids, d)
    own, first, second = tie(own, first, second)
    parts = [
        sum(wider(block) for block in blocks).reshape(4, 4, size, cols)
        for blocks in zip(own, first, second)
    ]
    pair, single = jnp.stack(parts[:2]), parts[2][None]
    for phase, dtype in ((1, jnp.bfloat16), (0, jnp.float32)):
        out = [
            [block[:, 0]] + [block[:, flip].astype(dtype) for flip in (1, 2, 3)]
            for block in (pair, single)
        ]
        out = tie(*out)
        pairs, singles = direct(*out, phase)
        pair = out[0][0] + wider(pairs[1]) + wider(pairs[2]) + wider(pairs[3])
        single = out[1][0] + wider(singles[1]) + wider(singles[2]) + wider(singles[3])
    return jnp.concatenate([pair.reshape(-1, cols), single.reshape(-1, cols)])


def solution(mesh):
    return jax.shard_map(
        shards,
        mesh=mesh,
        in_specs=(
            P("wide", "narrow"),
            P(None, ("narrow", "wide"), None),
            P(("narrow", "wide"), None),
        ),
        out_specs=P("wide", "narrow"),
        check_vma=False,
    )
```

```python
import functools

import jax
import jax.numpy as jnp
import numpy as np
from jax import lax
from jax.experimental import pallas as pl
from jax.experimental.pallas import tpu as pltpu
from jax.sharding import PartitionSpec as P

GRID = (2, 4, 2, 2, 4)
RINGS_A = (("z", "y"), ("y", "x"), ("x", "z"))
RINGS_B = (("x", "x"), ("z", "z"), ("y", "y"))
RING = (RINGS_A[2], RINGS_A[2], RINGS_B[2])
FIRST = ((1, 1), (3, 3), (1, 3))
SECOND = ((3, 3), (1, 1), (3, 1))
BOTH = ("wide", "narrow")


def partners(rings, flips):
    pairs = []
    for place in np.ndindex(*GRID):
        zh, x, core, zl, y = place
        ring, flip = rings[core], flips[core]
        if ring == "z":
            z = (2 * zh + zl) ^ flip
            zh, zl = z // 2, z % 2
        elif ring == "x":
            x ^= flip
        elif ring == "y":
            y ^= flip
        else:
            core ^= flip
        pairs.append(
            (
                int(np.ravel_multi_index(place, GRID)),
                int(np.ravel_multi_index((zh, x, core, zl, y), GRID)),
            )
        )
    return pairs


def swap(block, rings, flips):
    return lax.ppermute(block, BOTH, partners(rings, flips))


def tie(*blocks):
    return lax.optimization_barrier(blocks)


def direct(pair, single, phase):
    pairs, singles = {}, {}
    for flip in (2, 1, 3):
        pairs[flip] = swap(pair[flip], RINGS_A[phase], (flip, flip))
    for flip in (2, 3):
        singles[flip] = swap(single[flip], RINGS_B[phase], (flip, flip))
    last, pairs[1] = tie(single[1], pairs[1])
    singles[1] = swap(last, RINGS_B[phase], (1, 1))
    return pairs, singles


VMEM_LIMIT = 10 * 2**20


def column_block(place, step):
    return (place[1] ^ (step // 4)) * 4 + (place[2] ^ (step % 4))


def resident(block):
    return pltpu.with_memory_space_constraint(block, pltpu.VMEM)


class Work:
    def __init__(self, places, hidden, output):
        self.places, self.hidden, self.output = places, hidden, output
        self.fresh = hidden and places == (0,)
        self.far = places == (2,)
        self.final = hidden and not self.fresh

    def __call__(self, place, tokens, gate_up, sums, hids, down, *after):
        width, cols = (down or gate_up)[0].shape[-2], (down or gate_up)[0].shape[-1] // 8
        self.width, self.cols = width, cols
        size = self.size
        total = 24 * size
        count = 3 * len(self.places)
        aliases = {}
        operands, out_shape, scratch = [place], [], []
        sum_shape = jax.ShapeDtypeStruct((4, total, width), jnp.float32)
        hid_shape = jax.ShapeDtypeStruct((total, width), jnp.bfloat16)
        if self.hidden:
            operands += [resident(block) for block in tokens]
            operands += [resident(block) for block in gate_up]
            if not self.fresh:
                aliases[len(operands)] = 0
                operands.append(resident(sums))
            scratch.append(pltpu.VMEM((1, total, cols), jnp.bfloat16))
            out_shape.append(sum_shape)
            if self.final:
                out_shape += [hid_shape, hid_shape]
        if self.output:
            operands += [resident(block) for block in (*down, *hids)]
            out_shape += [jax.ShapeDtypeStruct((16, size, cols), jnp.bfloat16)] * count
        operands += after
        self.after = len(after)
        vmem = pl.BlockSpec(memory_space=pltpu.VMEM)
        return pl.pallas_call(
            self.kernel,
            out_shape=out_shape,
            in_specs=[pl.BlockSpec(memory_space=pltpu.SMEM)] + [vmem] * (len(operands) - 1),
            out_specs=[vmem] * len(out_shape),
            scratch_shapes=scratch,
            input_output_aliases=aliases,
            compiler_params=pltpu.CompilerParams(vmem_limit_bytes=VMEM_LIMIT),
            cost_estimate=pl.CostEstimate(flops=2**36, bytes_accessed=2**27, transcendentals=0),
        )(*operands)

    def kernel(self, *refs):
        refs = list(refs)

        def take(count):
            taken = refs[:count]
            del refs[:count]
            return taken

        count = 3 * len(self.places)
        (place,) = take(1)
        if self.hidden:
            tokens, gate_up = take(count), take(2)
            if not self.fresh:
                take(1)
        if self.output:
            down = take(2)
            if not self.hidden:
                hids, late = take(2), take(2)
        take(self.after)
        if self.hidden:
            (sums,) = take(1)
            if self.final:
                new = take(2)
        if self.output:
            outs = take(count)
            if self.hidden:
                hids = late = new
        if self.hidden:
            (rows_k,) = take(1)

        def where(step):
            return pl.ds(pl.multiple_of(column_block(place, step) * self.cols, self.cols), self.cols)

        if self.fresh:
            sums[...] = jnp.zeros_like(sums)

        def run(core):
            steps = self.steps(core)
            if self.hidden:
                for step in steps:
                    self.hidden_step(core, step, tokens, gate_up, where(step), rows_k, sums)
            if self.final:
                for first, count in self.finished(core):
                    rows = pl.ds(first * self.size, count * self.size)
                    for part, h in enumerate(new):
                        gate, up = sums[2 * part, rows, :], sums[2 * part + 1, rows, :]
                        h[rows, :] = (gate / (1 + jnp.exp(-gate)) * up).astype(jnp.bfloat16)
            if self.output:
                for step in steps:
                    self.output_step(core, step, hids, late, down, where(step), outs)

        for core in range(2):
            pl.when(place[0] == core)(functools.partial(run, core))

    def steps(self, core):
        used = lambda zl, y: core == 0 or zl == self.places[0] % 2 or y in self.places
        return [4 * zl + y for zl in range(2) for y in range(4) if used(zl, y)]

    def finished(self, core):
        if self.far:
            return [(4, 2), (12, 2), (16, 8)] if core == 0 else [(4, 4), (12, 12)]
        return [(0, 4), (6, 6), (14, 2)] if core == 0 else [(0, 4), (8, 4)]

    def spans(self, core, step):
        zl, y = step // 4, step % 4
        found = []
        for stream in range(3):
            places = self.places
            if len(places) == 2:
                places = FIRST[stream][core], SECOND[stream][core]
            for i, near in enumerate(places):
                which = stream * len(places) + i
                if stream == 2:
                    if near == y:
                        blocks = [(2 * zh + zl) * 4 + x for zh in range(2) for x in range(4)]
                        found.append((which, 16, blocks))
                elif core == 0:
                    blocks = [y * 4 + 2 * zh + zl for zh in range(2)]
                    found.append((which, 8 * stream + 2 * near, blocks))
                elif near % 2 == zl:
                    blocks = [x * 4 + y for x in range(4)]
                    found.append((which, 8 * stream + 4 * (near // 2), blocks))
        return found

    def hidden_step(self, core, step, tokens, gate_up, cols, rows_k, sums):
        slot, row, size, runs = 0, 0, self.size, []
        for which, first, blocks in self.spans(core, step):
            runs.append((row, first * size, size * len(blocks)))
            for index in blocks:
                rows_k[slot, pl.ds(row, size), :] = tokens[which][index]
                row += size
        lhs = rows_k[slot, pl.ds(0, row), :]
        for part in range(2):
            for which in range(2):
                value = lax.dot_general(
                    lhs,
                    gate_up[part][which, :, cols],
                    (((1,), (1,)), ((), ())),
                    preferred_element_type=jnp.float32,
                )
                for start, first, count in runs:
                    sums[2 * part + which, pl.ds(first, count), :] += value[start : start + count]

    def output_step(self, core, step, hids, late, down, cols, outs):
        size = self.size
        spans, lhs = self.spans(core, step), ([], [])
        for _, first, blocks in spans:
            rows = pl.ds(first * size, size * len(blocks))
            is_late = any(begin <= first < begin + count for begin, count in FAR.finished(core))
            for part, hid in enumerate(late if is_late else hids):
                lhs[part].append(hid[rows, :])
        value = sum(
            jnp.dot(jnp.concatenate(rows), down[part][:, cols], preferred_element_type=jnp.float32)
            for part, rows in enumerate(lhs)
        )
        row = 0
        for which, _, blocks in spans:
            for index in blocks:
                outs[which][index] = value[row : row + size].astype(jnp.bfloat16)
                row += size


FAR = Work((2,), True, True)


def add_kernel(*refs):
    count = len(refs) // 3
    for block, other, out in zip(refs[:count], refs[count:], refs[2 * count :]):
        total = block[...].astype(jnp.float32) + other[...].astype(jnp.float32)
        out[...] = total.astype(jnp.bfloat16)


def add(blocks, others):
    count, rows, cols = blocks[0].shape
    spec = pl.BlockSpec((count // 4, rows, cols), lambda n: (n, 0, 0))
    return pl.pallas_call(
        add_kernel,
        out_shape=[jax.ShapeDtypeStruct(block.shape, block.dtype) for block in blocks],
        grid=(4,),
        in_specs=[spec] * (2 * len(blocks)),
        out_specs=[spec] * len(blocks),
        input_output_aliases={i: i for i in range(len(blocks))},
        compiler_params=pltpu.CompilerParams(vmem_limit_bytes=VMEM_LIMIT),
    )(*blocks, *others)


def wider(block):
    return block.astype(jnp.float32)


def each(blocks, flips):
    return [swap(block, ring, flip) for block, ring, flip in zip(blocks, RING, flips)]


def shards(tokens, gate_up, down_weight):
    index = lax.axis_index("wide"), lax.axis_index("narrow")
    place = jnp.stack([index[0] % 2, index[1] // 4, index[1] % 4]).astype(jnp.int32)
    rows, cols = tokens.shape
    Work.size = size = rows // 3
    cores = ("core", "core")
    w_other = swap(gate_up, cores, (1, 1))
    pair, single = tokens[: 2 * size].reshape(2, size, cols), tokens[2 * size :].reshape(1, size, cols)
    pairs, singles = direct([pair] * 4, [single] * 4, 0)
    pair = jnp.stack([pair] + [pairs[flip] for flip in (1, 2, 3)], axis=1)
    single = jnp.stack([single] + [singles[flip] for flip in (1, 2, 3)], axis=1)
    pair, single, arrived = tie(pair, single, w_other[0, :16, :128])
    w = gate_up, w_other
    pairs, singles = direct([pair] * 4, [single] * 4, 1)
    pairs, singles = [[own] + [got[flip] for flip in (1, 2, 3)] for own, got in ((pair, pairs), (single, singles))]
    own = [jnp.concatenate([block[i] for block in pairs]) for i in range(2)]
    own.append(jnp.concatenate([block[0] for block in singles]))
    own = list(tie(*own))

    first = each(own, FIRST)
    own_2, first[2] = tie(own[2], first[2])
    second = each([*own[:2], own_2], SECOND)
    (sums,) = Work((0,), True, False)(place, own, w, None, None, None, arrived)
    first[0], first[1], first[2], second[0], second[1], second[2], sums, down_weight = tie(
        *first, *second, sums, down_weight
    )
    relay = each(first, SECOND)
    d = down_weight, swap(down_weight, cores, (1, 1))
    near = [block for both in zip(first, second) for block in both]
    sums, *hids = Work((1, 3), True, False)(place, near, w, sums, None, None)
    *relay, sums = tie(*relay, sums)
    _, own_hid, other_hid, *far = FAR(place, relay, w, sums, [], d)
    hids += [own_hid, other_hid]

    arrived = each(far, FIRST)
    near = Work((1, 3), False, True)(place, None, None, None, hids, d)
    first, second = near[0::2], near[1::2]
    first = each(first, FIRST)
    second = each(add(second, arrived), SECOND)
    own = Work((0,), False, True)(place, None, None, None, hids, d)
    own, first, second = tie(own, first, second)
    parts = [
        sum(wider(block) for block in blocks).reshape(4, 4, size, cols)
        for blocks in zip(own, first, second)
    ]
    pair, single = jnp.stack(parts[:2]), parts[2][None]
    for phase, dtype in ((1, jnp.bfloat16), (0, jnp.float32)):
        out = [
            [block[:, 0]] + [block[:, flip].astype(dtype) for flip in (1, 2, 3)]
            for block in (pair, single)
        ]
        out[0] = list(tie(*out[0]))
        pairs, singles = direct(*out, phase)
        pair = out[0][0] + wider(pairs[1]) + wider(pairs[2]) + wider(pairs[3])
        single = out[1][0] + wider(singles[1]) + wider(singles[2]) + wider(singles[3])
    return jnp.concatenate([pair.reshape(-1, cols), single.reshape(-1, cols)])


def solution(mesh):
    return jax.shard_map(
        shards,
        mesh=mesh,
        in_specs=(
            P("wide", "narrow"),
            P(None, ("narrow", "wide"), None),
            P(("narrow", "wide"), None),
        ),
        out_specs=P("wide", "narrow"),
        check_vma=False,
    )
```
